32 devices in a mesh: blk: 4 (over y, x), grp: 8 (over z, core).
Axes of the slice: x: 2, y: 2, z: 4, core: 2. Of those that a mesh axis runs over, the one named last changes fastest.
Arguments:
- green_blocks: bfloat16 [96, 65536], P('blk', 'grp'), may hold values from -6 to 6
- chol_slab: bfloat16 [65536, 8192], P('grp', 'blk'), may hold values from -0.09375 to 0.09375
- aux_fields: bfloat16 [96, 8192], P('grp', 'blk'), may hold values from -6 to 6
Outputs:
- force_bias: float32 [96, 8192], P('grp', 'blk')
- field_term: bfloat16 [96, 65536], P('blk', 'grp')
The draws below stay inside these ranges and needn't reach their ends.
All inputs are finite; a program needn't handle non-finite values.
Results may differ from the reference program's by a relative error of at most 0.0049.
Values may be sent and summed in bfloat16 or wider, within the bound.
No kernel may reach another device: no remote copies, remote signals or barrier semaphores. Data moves between devices by JAX's collectives and lax.ppermute only.
A program may use at most 64 MiB of HBM per device.

```python
import jax
import jax.numpy as jnp
from jax import lax

NCHOL = 8192
WALKERS = 96
ROWS = 65536


def block_levels(rng, dims, shards, least, largest):
    def one(axis_at, shards_of):
        steps = jax.random.uniform(jax.random.fold_in(jax.random.fold_in(rng, 6), axis_at), (shards_of,), jnp.float32, least / len(shards), largest / len(shards))
        return jnp.repeat(jnp.exp(steps), dims[axis_at] // shards_of).reshape((-1,) + (1,) * (len(dims) - axis_at - 1))

    gain = one(*shards[0])
    for cut in shards[1:]:
        gain = gain * one(*cut)
    return gain


def bell_draw(own_key, extent, spread, reach, cuts=(), held_as=jnp.bfloat16):
    entries = jax.random.normal(own_key, extent, jnp.float32) * spread
    if len(cuts) > 0:
        entries = block_levels(own_key, extent, cuts, -0.22, 0.18) * entries
    return jnp.clip(entries, min=-reach, max=reach).astype(held_as)


def setup_inputs(seed: int = 0) -> dict:
    streams_of = jax.random.split(jax.random.key(seed), 4)
    green_blocks = bell_draw(streams_of[0], (WALKERS, ROWS), 1.0, 6.0, ((0, 4), (1, 8)))
    chol_slab = bell_draw(streams_of[1], (ROWS, NCHOL), (ROWS // 16) ** -0.5, 0.09375, ((0, 8), (1, 4)))
    aux_fields = bell_draw(streams_of[2], (WALKERS, NCHOL), 1.0, 6.0, ((0, 8), (1, 4)))
    return dict(green_blocks=green_blocks, chol_slab=chol_slab, aux_fields=aux_fields)


tau_root = 0.1


def reference(green_blocks, chol_slab, aux_fields):
    force_bias = jnp.dot(green_blocks, chol_slab, preferred_element_type=jnp.float32)
    shifted = (aux_fields.astype(jnp.float32) + tau_root * force_bias).astype(jnp.bfloat16)
    field_term = lax.dot_general(shifted, chol_slab, (((1,), (1,)), ((), ())), preferred_element_type=jnp.float32)
    return force_bias, field_term.astype(jnp.bfloat16)
```

```python
import jax
import jax.numpy as jnp
from jax import lax
from jax.experimental import pallas as pl
from jax.experimental.pallas import tpu as pltpu
from jax.sharding import PartitionSpec as P

tau_root = 0.1
f32, bf16 = jnp.float32, jnp.bfloat16
VMEM = pl.BlockSpec(memory_space=pltpu.VMEM)
PAD = 32


def general(green_blocks, chol_slab, aux_fields):
    partial_value = jnp.dot(
        lax.all_gather(green_blocks, "blk", axis=0, tiled=True),
        chol_slab,
        preferred_element_type=f32,
    )
    bias_own = lax.psum_scatter(partial_value, "grp", scatter_dimension=0, tiled=True)
    field_own = (aux_fields.astype(f32) + tau_root * bias_own).astype(bf16)
    field_all = lax.all_gather(field_own, "grp", axis=0, tiled=True)
    summed = lax.psum_scatter(
        lax.dot_general(
            field_all, chol_slab, (((1,), (1,)), ((), ())), preferred_element_type=f32
        ),
        "blk",
        scatter_dimension=0,
        tiled=True,
    )
    return bias_own, summed.astype(bf16)


def swap(x, axis, bit):
    n = lax.axis_size(axis)
    return lax.ppermute(x, axis, [(i, i ^ bit) for i in range(n)])


def call(body, outs, *args, mib=8, flops=0, nbytes=1 << 18, ins=None, scratch=()):
    return pl.pallas_call(
        body,
        out_shape=outs,
        in_specs=ins or [VMEM] * len(args),
        out_specs=jax.tree.map(lambda _: VMEM, outs),
        scratch_shapes=scratch,
        compiler_params=pltpu.CompilerParams(vmem_limit_bytes=mib << 20),
        cost_estimate=pl.CostEstimate(flops=flops, bytes_accessed=nbytes, transcendentals=0),
    )(*args)


def struct(shape, dtype):
    return jax.ShapeDtypeStruct(shape, dtype)


def load_chunk(chol, i, rows):
    cols = chol.shape[1]
    parts = 4
    step = rows // parts

    def body(c_ref, o_ref, sems):
        copies = [
            pltpu.make_async_copy(
                c_ref.at[pl.ds(i * rows + p * step, step)],
                o_ref.at[pl.ds(p * step, step)],
                sems.at[p],
            )
            for p in range(parts)
        ]
        for c in copies:
            c.start()
        for c in copies:
            c.wait()

    return call(
        body,
        pltpu.VMEM((rows, cols), chol.dtype),
        pltpu.with_memory_space_constraint(chol, pltpu.HBM),
        nbytes=2 * rows * cols * 2,
        ins=[pl.BlockSpec(memory_space=pl.ANY)],
        scratch=[pltpu.SemaphoreType.DMA((parts,))],
    )


def ids():
    blk, grp = lax.axis_index("blk"), lax.axis_index("grp")
    return blk, grp // 2, grp % 2


def fast(green, chol, aux):
    wb, depth = green.shape
    width = chol.shape[1]
    wg = aux.shape[0]
    half, hd = width // 2, depth // 2
    n_chunks = depth // width

    def split(g_ref, aux_ref, a_ref, b_ref, sent_ref, sems):
        copies = [
            pltpu.make_async_copy(g_ref.at[:, pl.ds(h * hd, hd)], r, sems.at[h])
            for h, r in enumerate((a_ref, b_ref))
        ]
        for c in copies:
            c.start()
        _, _, core = ids()
        sent_ref[...] = aux_ref[:, pl.ds(pl.multiple_of((1 - core) * half, half), half)]
        for c in copies:
            c.wait()

    ga, gb, aux_sent = call(
        split,
        (struct((wb, hd), bf16), struct((wb, hd), bf16), struct((wg, half), bf16)),
        green, aux,
        ins=[pl.BlockSpec(memory_space=pl.ANY), VMEM],
        scratch=[pltpu.SemaphoreType.DMA((2,))],
    )
    xb, ya = swap(gb, "blk", 1), swap(ga, "blk", 2)
    xa, yb = swap(ga, "blk", 1), swap(gb, "blk", 2)
    da, db = swap(ya, "blk", 1), swap(xb, "blk", 2)
    chunks = [load_chunk(chol, i, width) for i in range(n_chunks)]

    aux_got = swap(aux_sent, "grp", 1)

    def bias_half(all_ref, chunk_refs, offset):
        total = None
        for k, c in enumerate(chunk_refs):
            term = jnp.dot(
                all_ref[:, k * width : (k + 1) * width],
                c[:, pl.ds(pl.multiple_of(offset, half), half)],
                preferred_element_type=f32,
            )
            total = term if total is None else total + term
        return total

    def first(*refs):
        pieces, chunk_refs, (all_ref, sent_ref) = refs[:8], refs[8:-2], refs[-2:]
        blk, _, core = ids()
        for p in range(4):
            rows = pl.ds(p * PAD, wb)
            all_ref[rows, :hd] = pieces[2 * p][...]
            all_ref[rows, hd:] = pieces[2 * p + 1][...]
            all_ref[pl.ds(p * PAD + wb, PAD - wb), :] = jnp.zeros((PAD - wb, depth), bf16)
        total = bias_half(all_ref, chunk_refs, (1 - core) * half)
        for p in range(4):
            sent_ref[blk ^ p] = total[p * PAD : p * PAD + wb].astype(bf16)

    flops1 = 2 * 128 * depth * half
    g_all, sent = call(
        first,
        (struct((4 * PAD, depth), bf16), struct((4, wb, half), bf16)),
        ga, gb, xa, xb, ya, yb, da, db, *chunks,
        flops=flops1,
    )
    other = swap(sent, "grp", 1)

    def second(*refs):
        all_ref, chunk_refs, out_ref = refs[0], refs[1:-1], refs[-1]
        blk, _, core = ids()
        total = bias_half(all_ref, chunk_refs, core * half)
        for p in range(4):
            out_ref[blk ^ p] = total[p * PAD : p * PAD + wb]

    mine = call(second, struct((4, wb, half), f32), g_all, *chunks, flops=flops1)

    def combine(mine_ref, other_ref, keep_ref, *sent_refs):
        _, z, _ = ids()
        keep_ref[...] = mine_ref[z] + other_ref[z].astype(f32)
        for t, s in enumerate(sent_refs, 1):
            s[...] = (mine_ref[z ^ t] + other_ref[z ^ t].astype(f32)).astype(bf16)

    keep, *sums = call(
        combine, (struct((wb, half), f32),) + (struct((wb, half), bf16),) * 3, mine, other
    )
    sums = [swap(s, "grp", 2 * t) for t, s in enumerate(sums, 1)]

    def shift(keep_ref, r1, r2, r3, aux_ref, got_ref, bias_ref, give_ref, out_ref):
        _, _, core = ids()
        bias = keep_ref[...]
        for r in (r1, r2, r3):
            bias = bias + r[...].astype(f32)
        bias_ref[...] = bias
        give_ref[...] = jnp.where(core == 0, bias[wg:], bias[:wg])
        own = aux_ref[:, pl.ds(pl.multiple_of(core * half, half), half)].astype(f32)
        got = got_ref[...].astype(f32)
        top = jnp.where(core == 0, own, got)
        low = jnp.where(core == 0, got, own)
        out_ref[...] = (jnp.concatenate([top, low], 0) + tau_root * bias).astype(bf16)

    bias, give, shifted = call(
        shift,
        (struct((wb, half), f32), struct((wg, half), f32), struct((wb, half), bf16)),
        keep, *sums, aux, aux_got,
    )
    blocks = [shifted] + [swap(shifted, "grp", 2 * t) for t in (1, 2, 3)]
    bias_got = swap(give, "grp", 1)

    def arrange(*refs):
        ins, out_ref = refs[:4], refs[4]
        blk, z, _ = ids()
        for t in range(4):
            out_ref[z ^ t ^ blk, :wb] = ins[t][...]
            out_ref[t, wb:] = jnp.zeros((PAD - wb, half), bf16)

    s_mine = call(arrange, struct((4, PAD, half), bf16), *blocks)
    s_other = swap(s_mine, "grp", 1)

    def field(mine_ref, other_ref, ca, cb, sx, sy, xb_ref, ya_ref, own_a, own_b, all_ref):
        _, _, core = ids()
        for ref, at in ((mine_ref, core), (other_ref, 1 - core)):
            all_ref[:, pl.ds(pl.multiple_of(at * half, half), half)] = ref[...].reshape(4 * PAD, half)
        for c, own, s, two, left in ((ca, own_a, sx, 1, ya_ref), (cb, own_b, sy, 2, xb_ref)):
            total = lax.dot_general(
                all_ref[...], c[...], (((1,), (1,)), ((), ())), preferred_element_type=f32
            )
            block = [total[p * PAD : p * PAD + wb] for p in range(4)]
            own[...] = block[0]
            s[0] = block[3].astype(bf16)
            s[1] = block[two].astype(bf16)
            left[...] = block[3 - two]

    def forward(rx, ry, xb_ref, ya_ref, own_a, own_b, sx, sy, new_a, new_b):
        sx[...] = (xb_ref[...] + ry[0].astype(f32)).astype(bf16)
        sy[...] = (ya_ref[...] + rx[0].astype(f32)).astype(bf16)
        new_a[...] = own_a[...] + rx[1].astype(f32)
        new_b[...] = own_b[...] + ry[1].astype(f32)

    one32, one16 = struct((wb, width), f32), struct((wb, width), bf16)
    two16 = struct((2, wb, width), bf16)
    pairs = range(n_chunks // 2)
    stage = [
        call(
            field,
            (two16, two16, one32, one32, one32, one32),
            s_mine, s_other, chunks[2 * i], chunks[2 * i + 1],
            flops=4 * 128 * width * width,
            scratch=[pltpu.VMEM((4 * PAD, width), bf16)],
        )
        for i in pairs
    ]
    got = [(swap(s[0], "blk", 1), swap(s[1], "blk", 2)) for s in stage]
    stage = [
        call(forward, (one16, one16, one32, one32), *got[i], *stage[i][2:]) for i in pairs
    ]
    got = [(swap(s[0], "blk", 1), swap(s[1], "blk", 2)) for s in stage]

    def final(*refs):
        out_ref = refs[-1]
        for i in pairs:
            own_a, own_b, rx, ry = refs[4 * i : 4 * i + 4]
            at = 2 * i * width
            out_ref[:, at : at + width] = (own_a[...] + ry[...].astype(f32)).astype(bf16)
            at += width
            out_ref[:, at : at + width] = (own_b[...] + rx[...].astype(f32)).astype(bf16)

    result = call(
        final,
        struct((wb, depth), bf16),
        *[r for i in pairs for r in (*stage[i][2:], *got[i])],
    )

    def own_bias(bias_ref, got_ref, out_ref):
        _, _, core = ids()
        b = bias_ref[...]
        out_ref[:, pl.ds(pl.multiple_of(core * half, half), half)] = jnp.where(
            core == 0, b[:wg], b[wg:]
        )
        out_ref[:, pl.ds(pl.multiple_of((1 - core) * half, half), half)] = got_ref[...]

    bias_own = call(own_bias, struct((wg, width), f32), bias, bias_got)
    return bias_own, result


def solution(mesh):
    blk, grp = mesh.shape["blk"], mesh.shape["grp"]

    def local(green, chol, aux):
        plane = blk == 4 and grp == 8
        fits = chol.shape[0] % (2 * chol.shape[1]) == 0 and green.shape[0] == 2 * aux.shape[0]
        return (fast if plane and fits and green.shape[0] <= PAD else general)(green, chol, aux)

    placed = (P("blk", "grp"), P("grp", "blk"), P("grp", "blk"))
    return jax.shard_map(
        local,
        mesh=mesh,
        in_specs=placed,
        out_specs=(P("grp", "blk"), P("blk", "grp")),
        check_vma=False,
    )
```

```python
import functools

import jax
import jax.numpy as jnp
from jax import lax
from jax.experimental import pallas as pl
from jax.experimental.pallas import tpu as pltpu
from jax.sharding import PartitionSpec as P

tau_root = 0.1
f32, bf16 = jnp.float32, jnp.bfloat16
VMEM = pl.BlockSpec(memory_space=pltpu.VMEM)
PAD = 32


def general(green_blocks, chol_slab, aux_fields):
    partial_value = jnp.dot(
        lax.all_gather(green_blocks, "blk", axis=0, tiled=True),
        chol_slab,
        preferred_element_type=f32,
    )
    bias_own = lax.psum_scatter(partial_value, "grp", scatter_dimension=0, tiled=True)
    field_own = (aux_fields.astype(f32) + tau_root * bias_own).astype(bf16)
    field_all = lax.all_gather(field_own, "grp", axis=0, tiled=True)
    summed = lax.psum_scatter(
        lax.dot_general(
            field_all, chol_slab, (((1,), (1,)), ((), ())), preferred_element_type=f32
        ),
        "blk",
        scatter_dimension=0,
        tiled=True,
    )
    return bias_own, summed.astype(bf16)


def swap(x, axis, bit):
    n = lax.axis_size(axis)
    return lax.ppermute(x, axis, [(i, i ^ bit) for i in range(n)])


def cross(x, turn):
    blks, grps = lax.axis_size("blk"), lax.axis_size("grp")
    pairs = [
        (b * grps + g, (b ^ (1 + (g + turn) % 2)) * grps + g) for b in range(blks) for g in range(grps)
    ]
    return lax.ppermute(x, ("blk", "grp"), pairs)


def call(body, outs, *args, mib=8, flops=0, ins=None, scratch=(), aliases=None):
    return pl.pallas_call(
        body,
        out_shape=outs,
        in_specs=ins or [VMEM] * len(args),
        out_specs=jax.tree.map(lambda _: VMEM, outs),
        scratch_shapes=scratch,
        input_output_aliases=aliases or {},
        compiler_params=pltpu.CompilerParams(vmem_limit_bytes=mib << 20),
        cost_estimate=pl.CostEstimate(flops=flops, bytes_accessed=1 << 18, transcendentals=0),
    )(*args)


def struct(shape, dtype):
    return jax.ShapeDtypeStruct(shape, dtype)


HBM = pl.BlockSpec(memory_space=pl.ANY)


def in_hbm(x):
    return pltpu.with_memory_space_constraint(x, pltpu.HBM)


def in_vmem(x):
    return pltpu.with_memory_space_constraint(x, pltpu.VMEM)


def run(copies):
    for c in copies:
        c.start()
    for c in copies:
        c.wait()


def piece_copies(c_ref, o_ref, sems, i, parts=2):
    rows = o_ref.shape[0]
    step = rows // parts
    return [
        pltpu.make_async_copy(
            c_ref.at[pl.ds(i * rows + p * step, step)],
            o_ref.at[pl.ds(p * step, step)],
            sems.at[p],
        )
        for p in range(parts)
    ]


def load_pieces(chol, first, count, piece, after):
    def body(c_ref, _, *refs):
        run([c for j in range(count) for c in piece_copies(c_ref, refs[j], refs[count].at[j], first + j)])

    return call(
        body,
        [piece] * count,
        in_hbm(chol),
        after,
        flops=count * 2 * 10**9,
        ins=[HBM, HBM],
        scratch=[pltpu.SemaphoreType.DMA((count, 2))],
    )


def transposed(piece, *after):
    rows, cols = piece.shape
    tile = min(512, rows, cols)

    def body(c, *refs):
        o = refs[-1]

        @pl.loop(0, rows // tile)
        def _(r):
            at = pl.ds(pl.multiple_of(r * tile, tile), tile)
            for j in range(cols // tile):
                o[j * tile : (j + 1) * tile, at] = c[at, j * tile : (j + 1) * tile].T

    return call(
        body, pltpu.VMEM((cols, rows), bf16), piece, *after, mib=8, ins=[VMEM] + [HBM] * len(after)
    )


def ids():
    blk, grp = lax.axis_index("blk"), lax.axis_index("grp")
    return blk, grp // 2, grp % 2


def role(p, core):
    return jnp.where(core == 0, p, (p >> 1) | ((p & 1) << 1))


def fast(green, chol, aux):
    wb, depth = green.shape
    width = chol.shape[1]
    wg = aux.shape[0]
    half = width // 2
    n_chunks = depth // width
    n_pieces, rows = 2 * n_chunks, width // 2
    piece = pltpu.VMEM((rows, width), bf16)

    near = cross(green, 0)

    def begin(c_ref, aux_ref, g_ref, c0_ref, c1_ref, kept_ref, sent_ref, own_ref, sems):
        _, _, core = ids()
        at = [pl.ds(pl.multiple_of(c * half, half), half) for c in (core, 1 - core)]
        run(
            [
                pltpu.make_async_copy(aux_ref.at[:, at[0]], kept_ref, sems.at[2, 0]),
                pltpu.make_async_copy(aux_ref.at[:, at[1]], sent_ref, sems.at[2, 1]),
                pltpu.make_async_copy(g_ref, own_ref, sems.at[3, 0]),
            ]
            + piece_copies(c_ref, c0_ref, sems.at[0], 0)
            + piece_copies(c_ref, c1_ref, sems.at[1], 1)
        )

    c0, c1, aux_kept, aux_sent, own = call(
        begin,
        (
            piece,
            piece,
            struct((wg, half), bf16),
            struct((wg, half), bf16),
            pltpu.VMEM((wb, depth), bf16),
        ),
        in_hbm(chol), in_hbm(aux), in_hbm(green),
        flops=4 * 10**9,
        ins=[HBM] * 3,
        scratch=[pltpu.SemaphoreType.DMA((4, 2))],
    )
    side, far = cross(own, 1), cross(near, 1)
    pieces = [c0, c1, *load_pieces(chol, 2, n_pieces - 4, piece, aux_kept)]
    aux_got = swap(aux_sent, "grp", 1)

    def bias_half(all_ref, c_refs, offset, start=0):
        total = None
        for k, c in enumerate(c_refs, start):
            term = jnp.dot(
                all_ref[:, k * rows : (k + 1) * rows],
                c[:, pl.ds(pl.multiple_of(offset, half), half)],
                preferred_element_type=f32,
            )
            total = term if total is None else total + term
        return total

    early = n_chunks
    here = n_pieces - 2

    def first(*refs):
        parts, c_refs, c_ref = refs[:4], refs[4 : 4 + here], refs[4 + here]
        all_ref, sent_ref, part_ref, *last_refs, sems, total_ref = refs[5 + here :]
        copies = [
            c for j, r in enumerate(last_refs) for c in piece_copies(c_ref, r, sems.at[j], here + j)
        ]
        for c in copies:
            c.start()
        blk, _, core = ids()

        @pl.when(core < 2)
        def _():
            for p in range(4):
                at = pl.ds(p * PAD, wb)
                all_ref[at, :] = parts[p][...]
                all_ref[pl.ds(p * PAD + wb, PAD - wb), :] = jnp.zeros((PAD - wb, depth), bf16)
            part_ref[...] = bias_half(all_ref, c_refs[:early], core * half)
            total_ref[...] = bias_half(all_ref, c_refs, (1 - core) * half)

        for c in copies:
            c.wait()
        total = total_ref[...] + bias_half(all_ref, last_refs, (1 - core) * half, here)
        for p in range(4):
            sent_ref[blk ^ role(p, core)] = total[p * PAD : p * PAD + wb].astype(bf16)

    flops1 = 2 * 128 * depth * half
    g_all, sent, part, *last = call(
        first,
        (
            struct((4 * PAD, depth), bf16),
            struct((4, wb, half), bf16),
            struct((4 * PAD, half), f32),
            piece,
            piece,
        ),
        own, near, side, far, *pieces, in_hbm(chol),
        flops=flops1,
        ins=[VMEM] * (4 + here) + [HBM],
        scratch=[pltpu.SemaphoreType.DMA((2, 2)), pltpu.VMEM((4 * PAD, half), f32)],
    )
    pieces += last
    other = swap(sent, "grp", 1)

    def second(all_ref, part_ref, *refs):
        c_refs, out_ref = refs[:-1], refs[-1]
        blk, _, core = ids()
        total = part_ref[...] + bias_half(all_ref, c_refs, core * half, early)
        for p in range(4):
            out_ref[blk ^ role(p, core)] = total[p * PAD : p * PAD + wb]

    mine = call(second, struct((4, wb, half), f32), g_all, part, *pieces[early:], flops=flops1)

    def combine(mine_ref, other_ref, keep_ref, *sent_refs):
        _, z, _ = ids()
        keep_ref[...] = mine_ref[z] + other_ref[z].astype(f32)
        for t, s in enumerate(sent_refs, 1):
            s[...] = (mine_ref[z ^ t] + other_ref[z ^ t].astype(f32)).astype(bf16)

    keep, *sums = call(
        combine, (struct((wb, half), f32),) + (struct((wb, half), bf16),) * 3, mine, other
    )
    sums = [swap(s, "grp", 2 * t) for t, s in enumerate(sums, 1)]
    turned = []
    for k in range(4):
        turned.append(
            transposed(pieces[k], turned[-1] if turned else sums[0], *pieces[k + 1 :])
        )

    def shift(keep_ref, r1, r2, r3, aux_ref, got_ref, _, bias_ref, give_ref, out_ref):
        _, _, core = ids()
        bias = keep_ref[...]
        for r in (r1, r2, r3):
            bias = bias + r[...].astype(f32)
        bias_ref[...] = bias
        give_ref[...] = jnp.where(core == 0, bias[wg:], bias[:wg])
        own = aux_ref[...].astype(f32)
        got = got_ref[...].astype(f32)
        top = jnp.where(core == 0, own, got)
        low = jnp.where(core == 0, got, own)
        out_ref[...] = (jnp.concatenate([top, low], 0) + tau_root * bias).astype(bf16)

    bias, give, shifted = call(
        shift,
        (struct((wb, half), f32), struct((wg, half), f32), struct((wb, half), bf16)),
        keep, *sums, aux_kept, aux_got, turned[-1],
        ins=[VMEM] * 6 + [HBM],
    )
    turned.append(transposed(pieces[4], shifted, *pieces[5:]))
    turned.append(transposed(pieces[5], turned[-1], *pieces[6:]))
    turned.append(transposed(pieces[6], turned[-1], *pieces[7:]))
    blocks = [shifted] + [swap(shifted, "grp", 2 * t) for t in (1, 2, 3)]
    bias_got = swap(give, "grp", 1)

    def arrange(*refs):
        ins, out_ref = refs[:4], refs[5]
        blk, z, _ = ids()
        for t in range(4):
            out_ref[z ^ t ^ blk, :wb] = ins[t][...]
            out_ref[t, wb:] = jnp.zeros((PAD - wb, half), bf16)

    s_mine = call(arrange, struct((4, PAD, half), bf16), *blocks, turned[-1], ins=[VMEM] * 4 + [HBM])
    s_other = swap(s_mine, "grp", 1)
    turned.append(transposed(pieces[7], s_mine))
    n_turned = len(turned)

    groups = [range(n_pieces - 2, n_pieces), range(n_pieces // 2, n_pieces - 2), range(n_pieces // 2)]

    def field(group, mine_ref, other_ref, *refs):
        c_refs, (s_ref, pass_ref, own_ref, all_ref) = refs[: len(group)], refs[-4:]
        _, _, core = ids()
        for ref, at in ((mine_ref, core), (other_ref, 1 - core)):
            cols = pl.ds(pl.multiple_of(at * half, half), half)
            for p in range(4):
                all_ref[p * PAD : (p + 1) * PAD, cols] = ref[role(p, core)]
        for j, (k, c) in enumerate(zip(group, c_refs)):
            if k < n_turned:
                total = jnp.dot(all_ref[...], c[...], preferred_element_type=f32)
            else:
                total = lax.dot_general(
                    c[...], all_ref[...], (((1,), (1,)), ((), ())), preferred_element_type=f32
                ).T
            block = [total[p * PAD : p * PAD + wb] for p in range(4)]
            at = pl.ds(j * rows, rows)
            own_ref[:, at] = block[0]
            pass_ref[:, at] = block[1]
            s_ref[0, :, at] = block[3].astype(bf16)
            s_ref[1, :, at] = block[2].astype(bf16)

    def forward(*refs):
        out_ref, new_ref = refs[-2:]
        start = 0
        for j in range(len(refs) // 3):
            got_ref, pass_ref, own_ref = refs[3 * j : 3 * j + 3]
            at = pl.ds(start, own_ref.shape[1])
            start += own_ref.shape[1]
            out_ref[:, at] = (pass_ref[...] + got_ref[0].astype(f32)).astype(bf16)
            new_ref[:, at] = own_ref[...] + got_ref[1].astype(f32)

    right = turned + pieces[n_turned:]
    stage = []
    for group in groups:
        n = len(group) * rows
        sent, passed, mine = call(
            functools.partial(field, group),
            (struct((2, wb, n), bf16), struct((wb, n), f32), struct((wb, n), f32)),
            s_mine, s_other, *right[group.start : group.stop], turned[-1],
            flops=4 * 128 * width * width,
            ins=[VMEM] * (2 + len(group)) + [HBM],
            scratch=[pltpu.VMEM((4 * PAD, width), bf16)],
        )
        stage.append((cross(sent, 1), passed, mine))
    done = []
    for part in (stage[1:][::-1], stage[:1]):
        n = sum(s[2].shape[1] for s in part)
        sent, mine = call(
            forward, (struct((wb, n), bf16), struct((wb, n), f32)), *[r for s in part for r in s]
        )
        done += [mine, cross(sent, 0)]

    def final(mine_ref, got_ref, last_ref, last_got_ref, out_ref):
        n = mine_ref.shape[1]
        out_ref[:, :n] = (mine_ref[...] + got_ref[...].astype(f32)).astype(bf16)
        out_ref[:, n:] = (last_ref[...] + last_got_ref[...].astype(f32)).astype(bf16)

    result = call(final, struct((wb, depth), bf16), *done)

    def own_bias(bias_ref, got_ref, out_ref):
        _, _, core = ids()
        b = bias_ref[...]
        out_ref[:, pl.ds(pl.multiple_of(core * half, half), half)] = jnp.where(
            core == 0, b[:wg], b[wg:]
        )
        out_ref[:, pl.ds(pl.multiple_of((1 - core) * half, half), half)] = got_ref[...]

    bias_own = call(own_bias, struct((wg, width), f32), bias, bias_got)
    return bias_own, result


def solution(mesh):
    blk, grp = mesh.shape["blk"], mesh.shape["grp"]

    def local(green, chol, aux):
        plane = blk == 4 and grp == 8
        fits = chol.shape[0] % (2 * chol.shape[1]) == 0 and green.shape[0] == 2 * aux.shape[0]
        return (fast if plane and fits and green.shape[0] <= PAD else general)(green, chol, aux)

    placed = (P("blk", "grp"), P("grp", "blk"), P("grp", "blk"))
    return jax.shard_map(
        local,
        mesh=mesh,
        in_specs=placed,
        out_specs=(P("grp", "blk"), P("blk", "grp")),
        check_vma=False,
    )
```

```python
import functools

import jax
import jax.numpy as jnp
from jax import lax
from jax.experimental import pallas as pl
from jax.experimental.pallas import tpu as pltpu
from jax.sharding import PartitionSpec as P

tau_root = 0.1
f32, bf16 = jnp.float32, jnp.bfloat16
VMEM = pl.BlockSpec(memory_space=pltpu.VMEM)
PAD = 32


def general(green_blocks, chol_slab, aux_fields):
    partial_value = jnp.dot(
        lax.all_gather(green_blocks, "blk", axis=0, tiled=True),
        chol_slab,
        preferred_element_type=f32,
    )
    bias_own = lax.psum_scatter(partial_value, "grp", scatter_dimension=0, tiled=True)
    field_own = (aux_fields.astype(f32) + tau_root * bias_own).astype(bf16)
    field_all = lax.all_gather(field_own, "grp", axis=0, tiled=True)
    summed = lax.psum_scatter(
        lax.dot_general(
            field_all, chol_slab, (((1,), (1,)), ((), ())), preferred_element_type=f32
        ),
        "blk",
        scatter_dimension=0,
        tiled=True,
    )
    return bias_own, summed.astype(bf16)


def swap(x, axis, bit):
    n = lax.axis_size(axis)
    return lax.ppermute(x, axis, [(i, i ^ bit) for i in range(n)])


def cross(x, turn):
    blks, grps = lax.axis_size("blk"), lax.axis_size("grp")
    pairs = [
        (b * grps + g, (b ^ (1 + (g + turn) % 2)) * grps + g) for b in range(blks) for g in range(grps)
    ]
    return lax.ppermute(x, ("blk", "grp"), pairs)


def call(body, outs, *args, mib=4, flops=0, ins=None, scratch=(), aliases=None):
    return pl.pallas_call(
        body,
        out_shape=outs,
        in_specs=ins or [VMEM] * len(args),
        out_specs=jax.tree.map(lambda _: VMEM, outs),
        scratch_shapes=scratch,
        input_output_aliases=aliases or {},
        compiler_params=pltpu.CompilerParams(vmem_limit_bytes=mib << 20),
        cost_estimate=pl.CostEstimate(flops=flops, bytes_accessed=1 << 18, transcendentals=0),
    )(*args)


def struct(shape, dtype):
    return jax.ShapeDtypeStruct(shape, dtype)


HBM = pl.BlockSpec(memory_space=pl.ANY)


def in_hbm(x):
    return pltpu.with_memory_space_constraint(x, pltpu.HBM)


def in_vmem(x):
    return pltpu.with_memory_space_constraint(x, pltpu.VMEM)


def run(copies):
    for c in copies:
        c.start()
    for c in copies:
        c.wait()


def piece_copies(c_ref, o_ref, sems, i, parts=2):
    rows = o_ref.shape[0]
    step = rows // parts
    return [
        pltpu.make_async_copy(
            c_ref.at[pl.ds(i * rows + p * step, step)],
            o_ref.at[pl.ds(p * step, step)],
            sems.at[p],
        )
        for p in range(parts)
    ]


def load_pieces(chol, first, count, piece, after):
    def body(c_ref, _, *refs):
        run([c for j in range(count) for c in piece_copies(c_ref, refs[j], refs[count].at[j], first + j)])

    return call(
        body,
        [piece] * count,
        in_hbm(chol),
        after,
        flops=count * 2 * 10**9,
        ins=[HBM, HBM],
        scratch=[pltpu.SemaphoreType.DMA((count, 2))],
    )


def transposed(piece, *after):
    rows, cols = piece.shape
    tile = min(512, rows, cols)

    def body(c, *refs):
        o = refs[-1]

        @pl.loop(0, rows // tile)
        def _(r):
            at = pl.ds(pl.multiple_of(r * tile, tile), tile)
            for j in range(cols // tile):
                o[j * tile : (j + 1) * tile, at] = c[at, j * tile : (j + 1) * tile].T

    return call(
        body, pltpu.VMEM((cols, rows), bf16), piece, *after, mib=2, ins=[VMEM] + [HBM] * len(after)
    )


def ids():
    blk, grp = lax.axis_index("blk"), lax.axis_index("grp")
    return blk, grp // 2, grp % 2


def role(p, core):
    return jnp.where(core == 0, p, (p >> 1) | ((p & 1) << 1))


def fast(green, chol, aux):
    wb, depth = green.shape
    width = chol.shape[1]
    wg = aux.shape[0]
    half = width // 2
    n_chunks = depth // width
    n_pieces, rows = 2 * n_chunks, width // 2
    piece = pltpu.VMEM((rows, width), bf16)
    tile = min(256, half)

    near = cross(green, 0)

    def begin(c_ref, aux_ref, g_ref, c0_ref, c1_ref, kept_ref, sent_ref, own_ref, sems):
        _, _, core = ids()
        at = [pl.ds(pl.multiple_of(c * half, half), half) for c in (core, 1 - core)]
        run(
            [
                pltpu.make_async_copy(aux_ref.at[:, at[0]], kept_ref, sems.at[2, 0]),
                pltpu.make_async_copy(aux_ref.at[:, at[1]], sent_ref, sems.at[2, 1]),
                pltpu.make_async_copy(g_ref, own_ref, sems.at[3, 0]),
            ]
            + piece_copies(c_ref, c0_ref, sems.at[0], 0)
            + piece_copies(c_ref, c1_ref, sems.at[1], 1)
        )

    c0, c1, aux_kept, aux_sent, own = call(
        begin,
        (
            piece,
            piece,
            struct((wg, half), bf16),
            struct((wg, half), bf16),
            pltpu.VMEM((wb, depth), bf16),
        ),
        in_hbm(chol), in_hbm(aux), in_hbm(green),
        flops=4 * 10**9,
        ins=[HBM] * 3,
        scratch=[pltpu.SemaphoreType.DMA((4, 2))],
    )
    side, far = cross(own, 1), cross(near, 1)
    pieces = [c0, c1, *load_pieces(chol, 2, n_pieces - 4, piece, aux_kept)]
    aux_got = swap(aux_sent, "grp", 1)

    def bias_half(all_ref, c_refs, offset, start=0):
        for n in range(0, half, tile):
            total = None
            for k, c in enumerate(c_refs, start):
                term = jnp.dot(
                    all_ref[:, k * rows : (k + 1) * rows],
                    c[:, pl.ds(pl.multiple_of(offset + n, tile), tile)],
                    preferred_element_type=f32,
                )
                total = term if total is None else total + term
            yield slice(n, n + tile), total

    early = n_chunks
    here = n_pieces - 2

    def first(*refs):
        parts, c_refs, c_ref = refs[:4], refs[4 : 4 + here], refs[4 + here]
        all_ref, sent_ref, part_ref, *last_refs, sems, total_ref = refs[5 + here :]
        copies = [
            c for j, r in enumerate(last_refs) for c in piece_copies(c_ref, r, sems.at[j], here + j)
        ]
        for c in copies:
            c.start()
        blk, _, core = ids()

        @pl.when(core < 2)
        def _():
            for p in range(4):
                at = pl.ds(p * PAD, wb)
                all_ref[at, :] = parts[p][...]
                all_ref[pl.ds(p * PAD + wb, PAD - wb), :] = jnp.zeros((PAD - wb, depth), bf16)
            for at, total in bias_half(all_ref, c_refs[:early], core * half):
                part_ref[:, at] = total
            for at, total in bias_half(all_ref, c_refs, (1 - core) * half):
                total_ref[:, at] = total

        for c in copies:
            c.wait()
        for at, total in bias_half(all_ref, last_refs, (1 - core) * half, here):
            total += total_ref[:, at]
            for p in range(4):
                sent_ref[blk ^ role(p, core), :, at] = total[p * PAD : p * PAD + wb].astype(bf16)

    flops1 = 2 * 128 * depth * half
    g_all, sent, part, *last = call(
        first,
        (
            struct((4 * PAD, depth), bf16),
            struct((4, wb, half), bf16),
            struct((4 * PAD, half), f32),
            piece,
            piece,
        ),
        own, near, side, far, *pieces, in_hbm(chol),
        flops=flops1,
        ins=[VMEM] * (4 + here) + [HBM],
        scratch=[pltpu.SemaphoreType.DMA((2, 2)), pltpu.VMEM((4 * PAD, half), f32)],
    )
    pieces += last
    other = swap(sent, "grp", 1)

    def second(all_ref, part_ref, *refs):
        c_refs, out_ref = refs[:-1], refs[-1]
        blk, _, core = ids()
        for at, total in bias_half(all_ref, c_refs, core * half, early):
            total += part_ref[:, at]
            for p in range(4):
                out_ref[blk ^ role(p, core), :, at] = total[p * PAD : p * PAD + wb]

    mine = call(second, struct((4, wb, half), f32), g_all, part, *pieces[early:], flops=flops1)

    def combine(mine_ref, other_ref, keep_ref, *sent_refs):
        _, z, _ = ids()
        keep_ref[...] = mine_ref[z] + other_ref[z].astype(f32)
        for t, s in enumerate(sent_refs, 1):
            s[...] = (mine_ref[z ^ t] + other_ref[z ^ t].astype(f32)).astype(bf16)

    keep, *sums = call(
        combine, (struct((wb, half), f32),) + (struct((wb, half), bf16),) * 3, mine, other
    )
    sums = [swap(s, "grp", 2 * t) for t, s in enumerate(sums, 1)]
    turned = []
    for k in range(4):
        turned.append(
            transposed(pieces[k], turned[-1] if turned else sums[0], *pieces[k + 1 :])
        )

    def shift(keep_ref, r1, r2, r3, aux_ref, got_ref, _, bias_ref, give_ref, out_ref):
        _, _, core = ids()
        bias = keep_ref[...]
        for r in (r1, r2, r3):
            bias = bias + r[...].astype(f32)
        bias_ref[...] = bias
        give_ref[...] = jnp.where(core == 0, bias[wg:], bias[:wg])
        own = aux_ref[...].astype(f32)
        got = got_ref[...].astype(f32)
        top = jnp.where(core == 0, own, got)
        low = jnp.where(core == 0, got, own)
        out_ref[...] = (jnp.concatenate([top, low], 0) + tau_root * bias).astype(bf16)

    bias, give, shifted = call(
        shift,
        (struct((wb, half), f32), struct((wg, half), f32), struct((wb, half), bf16)),
        keep, *sums, aux_kept, aux_got, turned[-1],
        ins=[VMEM] * 6 + [HBM],
    )
    turned.append(transposed(pieces[4], shifted, *pieces[5:]))
    turned.append(transposed(pieces[5], turned[-1], *pieces[6:]))
    turned.append(transposed(pieces[6], turned[-1], *pieces[7:]))
    blocks = [shifted] + [swap(shifted, "grp", 2 * t) for t in (1, 2, 3)]
    bias_got = swap(give, "grp", 1)

    def arrange(*refs):
        ins, out_ref = refs[:4], refs[5]
        blk, z, _ = ids()
        for t in range(4):
            out_ref[z ^ t ^ blk, :wb] = ins[t][...]
            out_ref[t, wb:] = jnp.zeros((PAD - wb, half), bf16)

    s_mine = call(arrange, struct((4, PAD, half), bf16), *blocks, turned[-1], ins=[VMEM] * 4 + [HBM])
    s_other = swap(s_mine, "grp", 1)
    turned.append(transposed(pieces[7], s_mine))

    groups = [range(n_pieces - 2, n_pieces), range(n_pieces // 2, n_pieces - 2), range(n_pieces // 2)]

    def field(group, mine_ref, other_ref, *refs):
        c_refs, (s_ref, pass_ref, own_ref, all_ref) = refs[: len(group)], refs[-4:]
        _, _, core = ids()
        for ref, at in ((mine_ref, core), (other_ref, 1 - core)):
            cols = pl.ds(pl.multiple_of(at * half, half), half)
            for p in range(4):
                all_ref[p * PAD : (p + 1) * PAD, cols] = ref[role(p, core)]
        for j, c in enumerate(c_refs):
            for n in range(0, rows, tile):
                total = jnp.dot(all_ref[...], c[:, n : n + tile], preferred_element_type=f32)
                block = [total[p * PAD : p * PAD + wb] for p in range(4)]
                at = slice(j * rows + n, j * rows + n + tile)
                own_ref[:, at] = block[0]
                pass_ref[:, at] = block[1]
                s_ref[0, :, at] = block[3].astype(bf16)
                s_ref[1, :, at] = block[2].astype(bf16)

    def forward(*refs):
        out_ref, new_ref = refs[-2:]
        start = 0
        for j in range(len(refs) // 3):
            got_ref, pass_ref, own_ref = refs[3 * j : 3 * j + 3]
            at = pl.ds(start, own_ref.shape[1])
            start += own_ref.shape[1]
            out_ref[:, at] = (pass_ref[...] + got_ref[0].astype(f32)).astype(bf16)
            new_ref[:, at] = own_ref[...] + got_ref[1].astype(f32)

    stage = []
    for group in groups:
        n = len(group) * rows
        sent, passed, mine = call(
            functools.partial(field, group),
            (struct((2, wb, n), bf16), struct((wb, n), f32), struct((wb, n), f32)),
            s_mine, s_other, *turned[group.start : group.stop], turned[-1],
            flops=4 * 128 * width * width,
            ins=[VMEM] * (2 + len(group)) + [HBM],
            scratch=[pltpu.VMEM((4 * PAD, width), bf16)],
        )
        stage.append((cross(sent, 1), passed, mine))
    done = []
    for part in (stage[1:][::-1], stage[:1]):
        n = sum(s[2].shape[1] for s in part)
        sent, mine = call(
            forward, (struct((wb, n), bf16), struct((wb, n), f32)), *[r for s in part for r in s]
        )
        done += [mine, cross(sent, 0)]

    def final(mine_ref, got_ref, last_ref, last_got_ref, out_ref):
        n = mine_ref.shape[1]
        out_ref[:, :n] = (mine_ref[...] + got_ref[...].astype(f32)).astype(bf16)
        out_ref[:, n:] = (last_ref[...] + last_got_ref[...].astype(f32)).astype(bf16)

    result = call(final, struct((wb, depth), bf16), *done)

    def own_bias(bias_ref, got_ref, out_ref):
        _, _, core = ids()
        b = bias_ref[...]
        out_ref[:, pl.ds(pl.multiple_of(core * half, half), half)] = jnp.where(
            core == 0, b[:wg], b[wg:]
        )
        out_ref[:, pl.ds(pl.multiple_of((1 - core) * half, half), half)] = got_ref[...]

    bias_own = call(own_bias, struct((wg, width), f32), bias, bias_got)
    return bias_own, result


def solution(mesh):
    blk, grp = mesh.shape["blk"], mesh.shape["grp"]

    def local(green, chol, aux):
        plane = blk == 4 and grp == 8
        fits = chol.shape[0] % (2 * chol.shape[1]) == 0 and green.shape[0] == 2 * aux.shape[0]
        return (fast if plane and fits and green.shape[0] <= PAD else general)(green, chol, aux)

    placed = (P("blk", "grp"), P("grp", "blk"), P("grp", "blk"))
    return jax.shard_map(
        local,
        mesh=mesh,
        in_specs=placed,
        out_specs=(P("grp", "blk"), P("blk", "grp")),
        check_vma=False,
    )
```

```python
import functools

import jax
import jax.numpy as jnp
from jax import lax
from jax.experimental import pallas as pl
from jax.experimental.pallas import tpu as pltpu
from jax.sharding import PartitionSpec as P

tau_root = 0.1
f32, bf16 = jnp.float32, jnp.bfloat16
VMEM = pl.BlockSpec(memory_space=pltpu.VMEM)
PAD = 32


def general(green_blocks, chol_slab, aux_fields):
    partial_value = jnp.dot(
        lax.all_gather(green_blocks, "blk", axis=0, tiled=True),
        chol_slab,
        preferred_element_type=f32,
    )
    bias_own = lax.psum_scatter(partial_value, "grp", scatter_dimension=0, tiled=True)
    field_own = (aux_fields.astype(f32) + tau_root * bias_own).astype(bf16)
    field_all = lax.all_gather(field_own, "grp", axis=0, tiled=True)
    summed = lax.psum_scatter(
        lax.dot_general(
            field_all, chol_slab, (((1,), (1,)), ((), ())), preferred_element_type=f32
        ),
        "blk",
        scatter_dimension=0,
        tiled=True,
    )
    return bias_own, summed.astype(bf16)


def swap(x, axis, bit):
    n = lax.axis_size(axis)
    return lax.ppermute(x, axis, [(i, i ^ bit) for i in range(n)])


def cross(x, turn):
    blks, grps = lax.axis_size("blk"), lax.axis_size("grp")
    pairs = [
        (b * grps + g, (b ^ (1 + (g + turn) % 2)) * grps + g) for b in range(blks) for g in range(grps)
    ]
    return lax.ppermute(x, ("blk", "grp"), pairs)


def call(body, outs, *args, mib=3, flops=0, ins=None, scratch=(), aliases=None):
    return pl.pallas_call(
        body,
        out_shape=outs,
        in_specs=ins or [VMEM] * len(args),
        out_specs=jax.tree.map(lambda _: VMEM, outs),
        scratch_shapes=scratch,
        input_output_aliases=aliases or {},
        compiler_params=pltpu.CompilerParams(vmem_limit_bytes=mib << 20),
        cost_estimate=pl.CostEstimate(flops=flops, bytes_accessed=1 << 18, transcendentals=0),
    )(*args)


def struct(shape, dtype):
    return jax.ShapeDtypeStruct(shape, dtype)


HBM = pl.BlockSpec(memory_space=pl.ANY)


def in_hbm(x):
    return pltpu.with_memory_space_constraint(x, pltpu.HBM)


def in_vmem(x):
    return pltpu.with_memory_space_constraint(x, pltpu.VMEM)


def run(copies):
    for c in copies:
        c.start()
    for c in copies:
        c.wait()


def piece_copies(c_ref, o_ref, sems, i, parts=2):
    rows = o_ref.shape[0]
    step = rows // parts
    return [
        pltpu.make_async_copy(
            c_ref.at[pl.ds(i * rows + p * step, step)],
            o_ref.at[pl.ds(p * step, step)],
            sems.at[p],
        )
        for p in range(parts)
    ]


def load_pieces(chol, first, count, piece, after):
    def body(c_ref, _, *refs):
        run([c for j in range(count) for c in piece_copies(c_ref, refs[j], refs[count].at[j], first + j)])

    return call(
        body,
        [piece] * count,
        in_hbm(chol),
        after,
        flops=count * 2 * 10**9,
        ins=[HBM, HBM],
        scratch=[pltpu.SemaphoreType.DMA((count, 2))],
    )


def transposed(piece, *after):
    rows, cols = piece.shape
    tile = min(512, rows, cols)

    def body(c, *refs):
        o = refs[-1]

        @pl.loop(0, rows // tile)
        def _(r):
            at = pl.ds(pl.multiple_of(r * tile, tile), tile)
            for j in range(cols // tile):
                o[j * tile : (j + 1) * tile, at] = c[at, j * tile : (j + 1) * tile].T

    return call(
        body, pltpu.VMEM((cols, rows), bf16), piece, *after, mib=2, ins=[VMEM] + [HBM] * len(after)
    )


def ids():
    blk, grp = lax.axis_index("blk"), lax.axis_index("grp")
    return blk, grp // 2, grp % 2


def role(p, core):
    return jnp.where(core == 0, p, (p >> 1) | ((p & 1) << 1))


def fast(green, chol, aux):
    wb, depth = green.shape
    width = chol.shape[1]
    wg = aux.shape[0]
    half = width // 2
    n_chunks = depth // width
    n_pieces, rows = 2 * n_chunks, width // 2
    piece = pltpu.VMEM((rows, width), bf16)
    tile = min(256, half)

    near = cross(green, 0)

    def begin(c_ref, aux_ref, g_ref, c0_ref, c1_ref, kept_ref, sent_ref, own_ref, sems):
        _, _, core = ids()
        at = [pl.ds(pl.multiple_of(c * half, half), half) for c in (core, 1 - core)]
        run(
            [
                pltpu.make_async_copy(aux_ref.at[:, at[0]], kept_ref, sems.at[2, 0]),
                pltpu.make_async_copy(aux_ref.at[:, at[1]], sent_ref, sems.at[2, 1]),
                pltpu.make_async_copy(g_ref, own_ref, sems.at[3, 0]),
            ]
            + piece_copies(c_ref, c0_ref, sems.at[0], 0)
            + piece_copies(c_ref, c1_ref, sems.at[1], 1)
        )

    c0, c1, aux_kept, aux_sent, own = call(
        begin,
        (
            piece,
            piece,
            struct((wg, half), bf16),
            struct((wg, half), bf16),
            pltpu.VMEM((wb, depth), bf16),
        ),
        in_hbm(chol), in_hbm(aux), in_hbm(green),
        flops=4 * 10**9,
        ins=[HBM] * 3,
        scratch=[pltpu.SemaphoreType.DMA((4, 2))],
    )
    side, far = cross(own, 1), cross(near, 1)
    pieces = [c0, c1, *load_pieces(chol, 2, n_pieces - 4, piece, aux_kept)]
    aux_got = swap(aux_sent, "grp", 1)

    def bias_half(all_ref, c_refs, offset, start=0):
        for n in range(0, half, tile):
            total = None
            for k, c in enumerate(c_refs, start):
                term = jnp.dot(
                    all_ref[:, k * rows : (k + 1) * rows],
                    c[:, pl.ds(pl.multiple_of(offset + n, tile), tile)],
                    preferred_element_type=f32,
                )
                total = term if total is None else total + term
            yield slice(n, n + tile), total

    early = n_chunks
    here = n_pieces - 2

    def first(*refs):
        parts, c_refs, c_ref = refs[:4], refs[4 : 4 + here], refs[4 + here]
        all_ref, sent_ref, part_ref, *last_refs, sems, total_ref = refs[5 + here :]
        copies = [
            c for j, r in enumerate(last_refs) for c in piece_copies(c_ref, r, sems.at[j], here + j)
        ]
        for c in copies:
            c.start()
        blk, _, core = ids()

        @pl.when(core < 2)
        def _():
            for p in range(4):
                at = pl.ds(p * PAD, wb)
                all_ref[at, :] = parts[p][...]
                all_ref[pl.ds(p * PAD + wb, PAD - wb), :] = jnp.zeros((PAD - wb, depth), bf16)
            for at, total in bias_half(all_ref, c_refs[:early], core * half):
                part_ref[:, at] = total
            for at, total in bias_half(all_ref, c_refs, (1 - core) * half):
                total_ref[:, at] = total

        for c in copies:
            c.wait()
        for at, total in bias_half(all_ref, last_refs, (1 - core) * half, here):
            total += total_ref[:, at]
            for p in range(4):
                sent_ref[blk ^ role(p, core), :, at] = total[p * PAD : p * PAD + wb].astype(bf16)

    flops1 = 2 * 128 * depth * half
    g_all, sent, part, *last = call(
        first,
        (
            struct((4 * PAD, depth), bf16),
            struct((4, wb, half), bf16),
            struct((4 * PAD, half), f32),
            piece,
            piece,
        ),
        own, near, side, far, *pieces, in_hbm(chol),
        flops=flops1,
        ins=[VMEM] * (4 + here) + [HBM],
        scratch=[pltpu.SemaphoreType.DMA((2, 2)), pltpu.VMEM((4 * PAD, half), f32)],
    )
    pieces += last
    other = swap(sent, "grp", 1)

    def second(all_ref, part_ref, *refs):
        c_refs, out_ref = refs[:-1], refs[-1]
        blk, _, core = ids()
        for at, total in bias_half(all_ref, c_refs, core * half, early):
            total += part_ref[:, at]
            for p in range(4):
                out_ref[blk ^ role(p, core), :, at] = total[p * PAD : p * PAD + wb]

    mine = call(second, struct((4, wb, half), f32), g_all, part, *pieces[early:], flops=flops1)

    def combine(mine_ref, other_ref, keep_ref, *sent_refs):
        _, z, _ = ids()
        keep_ref[...] = mine_ref[z] + other_ref[z].astype(f32)
        for t, s in zip((2, 3, 1), sent_refs):
            s[...] = (mine_ref[z ^ t] + other_ref[z ^ t].astype(f32)).astype(bf16)

    keep, *sums = call(
        combine, (struct((wb, half), f32),) + (struct((wb, half), bf16),) * 3, mine, other
    )
    sums = [swap(s, "grp", 2 * t) for t, s in zip((2, 3, 1), sums)]
    turned = []
    for k in range(3):
        turned.append(
            transposed(pieces[k], turned[-1] if turned else keep, *pieces[k + 1 :])
        )

    def shift(keep_ref, r1, r2, r3, aux_ref, got_ref, _, bias_ref, give_ref, out_ref):
        _, _, core = ids()
        bias = keep_ref[...]
        for r in (r1, r2, r3):
            bias = bias + r[...].astype(f32)
        bias_ref[...] = bias
        give_ref[...] = jnp.where(core == 0, bias[wg:], bias[:wg])
        own = aux_ref[...].astype(f32)
        got = got_ref[...].astype(f32)
        top = jnp.where(core == 0, own, got)
        low = jnp.where(core == 0, got, own)
        out_ref[...] = (jnp.concatenate([top, low], 0) + tau_root * bias).astype(bf16)

    bias, give, shifted = call(
        shift,
        (struct((wb, half), f32), struct((wg, half), f32), struct((wb, half), bf16)),
        keep, *sums, aux_kept, aux_got, turned[-1],
        ins=[VMEM] * 6 + [HBM],
    )
    for k in range(3, 6):
        turned.append(transposed(pieces[k], shifted if k == 3 else turned[-1], *pieces[k + 1 :]))
    blocks = [shifted] + [swap(shifted, "grp", 2 * t) for t in (1, 2, 3)]
    bias_got = swap(give, "grp", 1)

    def arrange(*refs):
        ins, out_ref = refs[:4], refs[5]
        blk, z, _ = ids()
        for t in range(4):
            out_ref[z ^ t ^ blk, :wb] = ins[t][...]
            out_ref[t, wb:] = jnp.zeros((PAD - wb, half), bf16)

    s_mine = call(arrange, struct((4, PAD, half), bf16), *blocks, turned[-1], ins=[VMEM] * 4 + [HBM])
    s_other = swap(s_mine, "grp", 1)

    n_first = n_pieces // 2
    groups = [range(n_first), range(n_first, n_pieces - 2), range(n_pieces - 2, n_pieces)]

    def placed(all_ref, ref, start):
        _, _, core = ids()
        for p in range(4):
            all_ref[p * PAD : (p + 1) * PAD, pl.ds(start, half)] = ref[role(p, core)]

    def tiles(c_refs):
        return [(c, n, slice(j * rows + n, j * rows + n + tile)) for j, c in enumerate(c_refs) for n in range(0, rows, tile)]

    def stored(total, at, s_ref, pass_ref, own_ref):
        block = [total[p * PAD : p * PAD + wb] for p in range(4)]
        own_ref[:, at] = block[0]
        pass_ref[:, at] = block[1]
        s_ref[0, :, at] = block[3].astype(bf16)
        s_ref[1, :, at] = block[2].astype(bf16)

    def field_mine(mine_ref, *refs):
        c_refs, (part_ref, all_ref) = refs[:-2], refs[-2:]
        _, _, core = ids()
        placed(all_ref, mine_ref, 0)
        k = pl.ds(pl.multiple_of(core * half, half), half)
        for c, n, at in tiles(c_refs):
            part_ref[:, at] = jnp.dot(all_ref[...], c[k, n : n + tile], preferred_element_type=f32)

    def field_other(other_ref, part_ref, *refs):
        c_refs, (*outs, all_ref) = refs[:-4], refs[-4:]
        _, _, core = ids()
        placed(all_ref, other_ref, 0)
        k = pl.ds(pl.multiple_of((1 - core) * half, half), half)
        for c, n, at in tiles(c_refs):
            total = jnp.dot(all_ref[...], c[k, n : n + tile], preferred_element_type=f32)
            stored(part_ref[:, at] + total, at, *outs)

    def field(group, mine_ref, other_ref, *refs):
        c_refs, (*outs, all_ref) = refs[: len(group)], refs[-4:]
        _, _, core = ids()
        placed(all_ref, mine_ref, pl.multiple_of(core * half, half))
        placed(all_ref, other_ref, pl.multiple_of((1 - core) * half, half))
        for c, n, at in tiles(c_refs):
            if group.start < len(turned):
                total = jnp.dot(all_ref[...], c[:, n : n + tile], preferred_element_type=f32)
            else:
                total = lax.dot_general(
                    c[n : n + tile, :], all_ref[...], (((1,), (1,)), ((), ())), preferred_element_type=f32
                ).T
            stored(total, at, *outs)

    def outs(group):
        n = len(group) * rows
        return struct((2, wb, n), bf16), struct((wb, n), f32), struct((wb, n), f32)

    some = [pltpu.VMEM((4 * PAD, half), bf16)]
    whole = [pltpu.VMEM((4 * PAD, width), bf16)]
    part = call(
        field_mine,
        struct((4 * PAD, n_first * rows), f32),
        s_mine, *turned[:n_first],
        scratch=some,
    )

    def later(group, after):
        n = len(group)
        return call(
            functools.partial(field, group),
            outs(group),
            s_mine, s_other, *(turned + pieces[len(turned) :])[group.start : group.stop], after,
            flops=4 * 128 * width * width,
            ins=[VMEM] * (2 + n) + [HBM],
            scratch=whole,
        )

    middle = later(groups[1], s_mine)
    last = later(groups[2], middle[2])
    opening = call(
        field_other,
        outs(groups[0]),
        s_other, part, *turned[:n_first],
        flops=4 * 128 * width * width,
        scratch=some,
    )
    stage = []
    for sent, passed, mine in (last, middle, opening):
        stage.append((cross(sent, 1), passed, mine))

    def forward(*refs):
        out_ref, new_ref = refs[-2:]
        start = 0
        for j in range(len(refs) // 3):
            got_ref, pass_ref, own_ref = refs[3 * j : 3 * j + 3]
            at = pl.ds(start, own_ref.shape[1])
            start += own_ref.shape[1]
            out_ref[:, at] = (pass_ref[...] + got_ref[0].astype(f32)).astype(bf16)
            new_ref[:, at] = own_ref[...] + got_ref[1].astype(f32)

    done = []
    for part in (stage[1:][::-1], stage[:1]):
        n = sum(s[2].shape[1] for s in part)
        sent, mine = call(
            forward, (struct((wb, n), bf16), struct((wb, n), f32)), *[r for s in part for r in s]
        )
        done += [mine, cross(sent, 0)]

    def final(mine_ref, got_ref, last_ref, last_got_ref, out_ref):
        n = mine_ref.shape[1]
        out_ref[:, :n] = (mine_ref[...] + got_ref[...].astype(f32)).astype(bf16)
        out_ref[:, n:] = (last_ref[...] + last_got_ref[...].astype(f32)).astype(bf16)

    result = call(final, struct((wb, depth), bf16), *done)

    def own_bias(bias_ref, got_ref, out_ref):
        _, _, core = ids()
        b = bias_ref[...]
        out_ref[:, pl.ds(pl.multiple_of(core * half, half), half)] = jnp.where(
            core == 0, b[:wg], b[wg:]
        )
        out_ref[:, pl.ds(pl.multiple_of((1 - core) * half, half), half)] = got_ref[...]

    bias_own = call(own_bias, struct((wg, width), f32), bias, bias_got)
    return bias_own, result


def solution(mesh):
    blk, grp = mesh.shape["blk"], mesh.shape["grp"]

    def local(green, chol, aux):
        plane = blk == 4 and grp == 8
        fits = chol.shape[0] % (2 * chol.shape[1]) == 0 and green.shape[0] == 2 * aux.shape[0]
        return (fast if plane and fits and green.shape[0] <= PAD else general)(green, chol, aux)

    placed = (P("blk", "grp"), P("grp", "blk"), P("grp", "blk"))
    return jax.shard_map(
        local,
        mesh=mesh,
        in_specs=placed,
        out_specs=(P("grp", "blk"), P("blk", "grp")),
        check_vma=False,
    )
```

```python
import functools

import jax
import jax.numpy as jnp
from jax import lax
from jax.experimental import pallas as pl
from jax.experimental.pallas import tpu as pltpu
from jax.sharding import PartitionSpec as P

tau_root = 0.1
f32, bf16 = jnp.float32, jnp.bfloat16
VMEM = pl.BlockSpec(memory_space=pltpu.VMEM)
PAD = 32


def general(green_blocks, chol_slab, aux_fields):
    partial_value = jnp.dot(
        lax.all_gather(green_blocks, "blk", axis=0, tiled=True),
        chol_slab,
        preferred_element_type=f32,
    )
    bias_own = lax.psum_scatter(partial_value, "grp", scatter_dimension=0, tiled=True)
    field_own = (aux_fields.astype(f32) + tau_root * bias_own).astype(bf16)
    field_all = lax.all_gather(field_own, "grp", axis=0, tiled=True)
    summed = lax.psum_scatter(
        lax.dot_general(
            field_all, chol_slab, (((1,), (1,)), ((), ())), preferred_element_type=f32
        ),
        "blk",
        scatter_dimension=0,
        tiled=True,
    )
    return bias_own, summed.astype(bf16)


def swap(x, axis, bit):
    n = lax.axis_size(axis)
    return lax.ppermute(x, axis, [(i, i ^ bit) for i in range(n)])


def cross(x, turn):
    blks, grps = lax.axis_size("blk"), lax.axis_size("grp")
    pairs = [
        (b * grps + g, (b ^ (1 + (g + turn) % 2)) * grps + g) for b in range(blks) for g in range(grps)
    ]
    return lax.ppermute(x, ("blk", "grp"), pairs)


def call(body, outs, *args, mib=3, flops=0, ins=None, scratch=(), aliases=None):
    return pl.pallas_call(
        body,
        out_shape=outs,
        in_specs=ins or [VMEM] * len(args),
        out_specs=jax.tree.map(lambda _: VMEM, outs),
        scratch_shapes=scratch,
        input_output_aliases=aliases or {},
        compiler_params=pltpu.CompilerParams(vmem_limit_bytes=mib << 20),
        cost_estimate=pl.CostEstimate(flops=flops, bytes_accessed=1 << 18, transcendentals=0),
    )(*args)


def struct(shape, dtype):
    return jax.ShapeDtypeStruct(shape, dtype)


HBM = pl.BlockSpec(memory_space=pl.ANY)


def in_hbm(x):
    return pltpu.with_memory_space_constraint(x, pltpu.HBM)


def in_vmem(x):
    return pltpu.with_memory_space_constraint(x, pltpu.VMEM)


def run(copies):
    for c in copies:
        c.start()
    for c in copies:
        c.wait()


def piece_copies(c_ref, o_ref, sems, i, parts=2):
    rows = o_ref.shape[0]
    step = rows // parts
    return [
        pltpu.make_async_copy(
            c_ref.at[pl.ds(i * rows + p * step, step)],
            o_ref.at[pl.ds(p * step, step)],
            sems.at[p],
        )
        for p in range(parts)
    ]


def load_pieces(chol, first, count, piece, after):
    def body(c_ref, _, *refs):
        run([c for j in range(count) for c in piece_copies(c_ref, refs[j], refs[count].at[j], first + j)])

    return call(
        body,
        [piece] * count,
        in_hbm(chol),
        after,
        flops=count * 2 * 10**9,
        ins=[HBM, HBM],
        scratch=[pltpu.SemaphoreType.DMA((count, 2))],
    )


def transposed(piece, *after):
    rows, cols = piece.shape
    tile = min(512, rows, cols)

    def body(c, *refs):
        o = refs[-1]

        @pl.loop(0, rows // tile)
        def _(r):
            at = pl.ds(pl.multiple_of(r * tile, tile), tile)
            for j in range(cols // tile):
                o[j * tile : (j + 1) * tile, at] = c[at, j * tile : (j + 1) * tile].T

    return call(
        body, pltpu.VMEM((cols, rows), bf16), piece, *after, mib=2, ins=[VMEM] + [HBM] * len(after)
    )


def ids():
    blk, grp = lax.axis_index("blk"), lax.axis_index("grp")
    return blk, grp // 2, grp % 2


def role(p, core):
    return jnp.where(core == 0, p, (p >> 1) | ((p & 1) << 1))


def fast(green, chol, aux):
    wb, depth = green.shape
    width = chol.shape[1]
    wg = aux.shape[0]
    half = width // 2
    n_chunks = depth // width
    n_pieces, rows = 2 * n_chunks, width // 2
    piece = pltpu.VMEM((rows, width), bf16)
    tile = min(256, half)

    near = cross(green, 0)

    def begin(c_ref, aux_ref, g_ref, c0_ref, c1_ref, kept_ref, sent_ref, own_ref, sems):
        _, _, core = ids()
        at = [pl.ds(pl.multiple_of(c * half, half), half) for c in (core, 1 - core)]
        run(
            [
                pltpu.make_async_copy(aux_ref.at[:, at[0]], kept_ref, sems.at[2, 0]),
                pltpu.make_async_copy(aux_ref.at[:, at[1]], sent_ref, sems.at[2, 1]),
                pltpu.make_async_copy(g_ref, own_ref, sems.at[3, 0]),
            ]
            + piece_copies(c_ref, c0_ref, sems.at[0], 0)
            + piece_copies(c_ref, c1_ref, sems.at[1], 1)
        )

    c0, c1, aux_kept, aux_sent, own = call(
        begin,
        (
            piece,
            piece,
            struct((wg, half), bf16),
            struct((wg, half), bf16),
            pltpu.VMEM((wb, depth), bf16),
        ),
        in_hbm(chol), in_hbm(aux), in_hbm(green),
        flops=4 * 10**9,
        ins=[HBM] * 3,
        scratch=[pltpu.SemaphoreType.DMA((4, 2))],
    )
    side, far = cross(own, 1), cross(near, 1)
    pieces = [c0, c1, *load_pieces(chol, 2, n_pieces - 4, piece, aux_kept)]
    aux_got = swap(aux_sent, "grp", 1)

    def bias_half(all_ref, c_refs, offset, start=0):
        for n in range(0, half, tile):
            total = None
            for k, c in enumerate(c_refs, start):
                term = jnp.dot(
                    all_ref[:, k * rows : (k + 1) * rows],
                    c[:, pl.ds(pl.multiple_of(offset + n, tile), tile)],
                    preferred_element_type=f32,
                )
                total = term if total is None else total + term
            yield slice(n, n + tile), total

    early = n_chunks
    here = n_pieces - 2

    def first(*refs):
        parts, c_refs, c_ref = refs[:4], refs[4 : 4 + here], refs[4 + here]
        all_ref, sent_ref, part_ref, *last_refs, sems, total_ref = refs[5 + here :]
        copies = [
            c for j, r in enumerate(last_refs) for c in piece_copies(c_ref, r, sems.at[j], here + j)
        ]
        for c in copies:
            c.start()
        blk, _, core = ids()

        @pl.when(core < 2)
        def _():
            for p in range(4):
                at = pl.ds(p * PAD, wb)
                all_ref[at, :] = parts[p][...]
                all_ref[pl.ds(p * PAD + wb, PAD - wb), :] = jnp.zeros((PAD - wb, depth), bf16)
            for at, total in bias_half(all_ref, c_refs[:early], core * half):
                part_ref[:, at] = total
            for at, total in bias_half(all_ref, c_refs, (1 - core) * half):
                total_ref[:, at] = total

        for c in copies:
            c.wait()
        for at, total in bias_half(all_ref, last_refs, (1 - core) * half, here):
            total += total_ref[:, at]
            for p in range(4):
                sent_ref[blk ^ role(p, core), :, at] = total[p * PAD : p * PAD + wb].astype(bf16)

    flops1 = 2 * 128 * depth * half
    g_all, sent, part, *last = call(
        first,
        (
            struct((4 * PAD, depth), bf16),
            struct((4, wb, half), bf16),
            struct((4 * PAD, half), f32),
            piece,
            piece,
        ),
        own, near, side, far, *pieces, in_hbm(chol),
        flops=flops1,
        ins=[VMEM] * (4 + here) + [HBM],
        scratch=[pltpu.SemaphoreType.DMA((2, 2)), pltpu.VMEM((4 * PAD, half), f32)],
    )
    pieces += last
    other = swap(sent, "grp", 1)

    def second(all_ref, part_ref, *refs):
        c_refs, out_ref = refs[:-1], refs[-1]
        blk, _, core = ids()
        for at, total in bias_half(all_ref, c_refs, core * half, early):
            total += part_ref[:, at]
            for p in range(4):
                out_ref[blk ^ role(p, core), :, at] = total[p * PAD : p * PAD + wb]

    mine = call(second, struct((4, wb, half), f32), g_all, part, *pieces[early:], flops=flops1)

    def combine(mine_ref, other_ref, keep_ref, *sent_refs):
        _, z, _ = ids()
        keep_ref[...] = mine_ref[z] + other_ref[z].astype(f32)
        for t, s in zip((2, 3, 1), sent_refs):
            s[...] = (mine_ref[z ^ t] + other_ref[z ^ t].astype(f32)).astype(bf16)

    keep, *sums = call(
        combine, (struct((wb, half), f32),) + (struct((wb, half), bf16),) * 3, mine, other
    )
    sums = [swap(s, "grp", 2 * t) for t, s in zip((2, 3, 1), sums)]
    turned = []
    for k in range(3):
        turned.append(
            transposed(pieces[k], turned[-1] if turned else keep, *pieces[k + 1 :])
        )

    def shift(keep_ref, r1, r2, r3, aux_ref, got_ref, _, bias_ref, give_ref, out_ref):
        _, _, core = ids()
        bias = keep_ref[...]
        for r in (r1, r2, r3):
            bias = bias + r[...].astype(f32)
        bias_ref[...] = bias
        give_ref[...] = jnp.where(core == 0, bias[wg:], bias[:wg])
        own = aux_ref[...].astype(f32)
        got = got_ref[...].astype(f32)
        top = jnp.where(core == 0, own, got)
        low = jnp.where(core == 0, got, own)
        out_ref[...] = (jnp.concatenate([top, low], 0) + tau_root * bias).astype(bf16)

    bias, give, shifted = call(
        shift,
        (struct((wb, half), f32), struct((wg, half), f32), struct((wb, half), bf16)),
        keep, *sums, aux_kept, aux_got, turned[-1],
        ins=[VMEM] * 6 + [HBM],
    )
    for k in range(3, 5):
        turned.append(transposed(pieces[k], shifted if k == 3 else turned[-1], *pieces[k + 1 :]))
    blocks = [shifted] + [swap(shifted, "grp", 2 * t) for t in (1, 2, 3)]
    bias_got = swap(give, "grp", 1)

    def arrange(*refs):
        ins, out_ref = refs[:4], refs[5]
        blk, z, _ = ids()
        for t in range(4):
            out_ref[z ^ t ^ blk, :wb] = ins[t][...]
            out_ref[t, wb:] = jnp.zeros((PAD - wb, half), bf16)

    s_mine = call(arrange, struct((4, PAD, half), bf16), *blocks, turned[-1], ins=[VMEM] * 4 + [HBM])
    s_other = swap(s_mine, "grp", 1)

    n_first = n_pieces // 2
    groups = [range(n_first), range(n_first, n_pieces - 2), range(n_pieces - 2, n_pieces)]

    def placed(all_ref, ref, start):
        _, _, core = ids()
        for p in range(4):
            all_ref[p * PAD : (p + 1) * PAD, pl.ds(start, half)] = ref[role(p, core)]

    def tiles(c_refs):
        return [
            (c, n, slice(j * rows + n, j * rows + n + tile))
            for j, c in enumerate(c_refs)
            for n in range(0, rows, tile)
        ]

    def stored(total, at, s_ref, pass_ref, own_ref):
        block = [total[p * PAD : p * PAD + wb] for p in range(4)]
        own_ref[:, at] = block[0]
        pass_ref[:, at] = block[1]
        s_ref[0, :, at] = block[3].astype(bf16)
        s_ref[1, :, at] = block[2].astype(bf16)

    def field_mine(mine_ref, *refs):
        c_refs, (part_ref, all_ref) = refs[:-2], refs[-2:]
        _, _, core = ids()
        placed(all_ref, mine_ref, 0)
        k = pl.ds(pl.multiple_of(core * half, half), half)
        for c, n, at in tiles(c_refs):
            part_ref[:, at] = jnp.dot(all_ref[...], c[k, n : n + tile], preferred_element_type=f32)

    def field_other(other_ref, part_ref, *refs):
        c_refs, (*outs, all_ref) = refs[:-4], refs[-4:]
        _, _, core = ids()
        placed(all_ref, other_ref, 0)
        k = pl.ds(pl.multiple_of((1 - core) * half, half), half)
        for c, n, at in tiles(c_refs):
            total = jnp.dot(all_ref[...], c[k, n : n + tile], preferred_element_type=f32)
            stored(part_ref[:, at] + total, at, *outs)

    def field(group, mine_ref, other_ref, *refs):
        c_refs, (*outs, all_ref) = refs[: len(group)], refs[-4:]
        _, _, core = ids()
        placed(all_ref, mine_ref, pl.multiple_of(core * half, half))
        placed(all_ref, other_ref, pl.multiple_of((1 - core) * half, half))
        for c, n, at in tiles(c_refs):
            if group.start + at.start // rows < len(turned):
                total = jnp.dot(all_ref[...], c[:, n : n + tile], preferred_element_type=f32)
            else:
                total = lax.dot_general(
                    c[n : n + tile, :], all_ref[...], (((1,), (1,)), ((), ())), preferred_element_type=f32
                ).T
            stored(total, at, *outs)

    def outs(group):
        n = len(group) * rows
        return struct((2, wb, n), bf16), struct((wb, n), f32), struct((wb, n), f32)

    some = [pltpu.VMEM((4 * PAD, half), bf16)]
    whole = [pltpu.VMEM((4 * PAD, width), bf16)]
    part = call(
        field_mine,
        struct((4 * PAD, n_first * rows), f32),
        s_mine, *turned[:n_first],
        scratch=some,
    )

    def later(group, after):
        n = len(group)
        return call(
            functools.partial(field, group),
            outs(group),
            s_mine, s_other, *(turned + pieces[len(turned) :])[group.start : group.stop], after,
            flops=4 * 128 * width * width,
            ins=[VMEM] * (2 + n) + [HBM],
            scratch=whole,
        )

    middle = later(groups[1], s_mine)
    last = later(groups[2], middle[2])
    opening = call(
        field_other,
        outs(groups[0]),
        s_other, part, *turned[:n_first],
        flops=4 * 128 * width * width,
        scratch=some,
    )
    stage = []
    for sent, passed, mine in (last, middle, opening):
        stage.append((cross(sent, 1), passed, mine))

    def forward(*refs):
        out_ref, new_ref = refs[-2:]
        start = 0
        for j in range(len(refs) // 3):
            got_ref, pass_ref, own_ref = refs[3 * j : 3 * j + 3]
            at = pl.ds(start, own_ref.shape[1])
            start += own_ref.shape[1]
            out_ref[:, at] = (pass_ref[...] + got_ref[0].astype(f32)).astype(bf16)
            new_ref[:, at] = own_ref[...] + got_ref[1].astype(f32)

    done = []
    for part in (stage[1:][::-1], stage[:1]):
        n = sum(s[2].shape[1] for s in part)
        sent, mine = call(
            forward, (struct((wb, n), bf16), struct((wb, n), f32)), *[r for s in part for r in s]
        )
        done += [mine, cross(sent, 0)]

    def final(mine_ref, got_ref, last_ref, last_got_ref, out_ref):
        n = mine_ref.shape[1]
        out_ref[:, :n] = (mine_ref[...] + got_ref[...].astype(f32)).astype(bf16)
        out_ref[:, n:] = (last_ref[...] + last_got_ref[...].astype(f32)).astype(bf16)

    result = call(final, struct((wb, depth), bf16), *done)

    def own_bias(bias_ref, got_ref, out_ref):
        _, _, core = ids()
        b = bias_ref[...]
        out_ref[:, pl.ds(pl.multiple_of(core * half, half), half)] = jnp.where(
            core == 0, b[:wg], b[wg:]
        )
        out_ref[:, pl.ds(pl.multiple_of((1 - core) * half, half), half)] = got_ref[...]

    bias_own = call(own_bias, struct((wg, width), f32), bias, bias_got)
    return bias_own, result


def solution(mesh):
    blk, grp = mesh.shape["blk"], mesh.shape["grp"]

    def local(green, chol, aux):
        plane = blk == 4 and grp == 8
        fits = chol.shape[0] % (2 * chol.shape[1]) == 0 and green.shape[0] == 2 * aux.shape[0]
        return (fast if plane and fits and green.shape[0] <= PAD else general)(green, chol, aux)

    placed = (P("blk", "grp"), P("grp", "blk"), P("grp", "blk"))
    return jax.shard_map(
        local,
        mesh=mesh,
        in_specs=placed,
        out_specs=(P("grp", "blk"), P("blk", "grp")),
        check_vma=False,
    )
```

```python
import functools

import jax
import jax.numpy as jnp
from jax import lax
from jax.experimental import pallas as pl
from jax.experimental.pallas import tpu as pltpu
from jax.sharding import PartitionSpec as P

tau_root = 0.1
f32, bf16 = jnp.float32, jnp.bfloat16
VMEM = pl.BlockSpec(memory_space=pltpu.VMEM)
PAD = 32


def general(green_blocks, chol_slab, aux_fields):
    partial_value = jnp.dot(
        lax.all_gather(green_blocks, "blk", axis=0, tiled=True),
        chol_slab,
        preferred_element_type=f32,
    )
    bias_own = lax.psum_scatter(partial_value, "grp", scatter_dimension=0, tiled=True)
    field_own = (aux_fields.astype(f32) + tau_root * bias_own).astype(bf16)
    field_all = lax.all_gather(field_own, "grp", axis=0, tiled=True)
    summed = lax.psum_scatter(
        lax.dot_general(
            field_all, chol_slab, (((1,), (1,)), ((), ())), preferred_element_type=f32
        ),
        "blk",
        scatter_dimension=0,
        tiled=True,
    )
    return bias_own, summed.astype(bf16)


def swap(x, axis, bit):
    n = lax.axis_size(axis)
    return lax.ppermute(x, axis, [(i, i ^ bit) for i in range(n)])


def cross(x, turn):
    blks, grps = lax.axis_size("blk"), lax.axis_size("grp")
    pairs = [
        (b * grps + g, (b ^ (1 + (g + turn) % 2)) * grps + g) for b in range(blks) for g in range(grps)
    ]
    return lax.ppermute(x, ("blk", "grp"), pairs)


def call(body, outs, *args, mib=3, flops=0, ins=None, scratch=(), aliases=None):
    return pl.pallas_call(
        body,
        out_shape=outs,
        in_specs=ins or [VMEM] * len(args),
        out_specs=jax.tree.map(lambda _: VMEM, outs),
        scratch_shapes=scratch,
        input_output_aliases=aliases or {},
        compiler_params=pltpu.CompilerParams(vmem_limit_bytes=mib << 20),
        cost_estimate=pl.CostEstimate(flops=flops, bytes_accessed=1 << 18, transcendentals=0),
    )(*args)


def struct(shape, dtype):
    return jax.ShapeDtypeStruct(shape, dtype)


HBM = pl.BlockSpec(memory_space=pl.ANY)


def in_hbm(x):
    return pltpu.with_memory_space_constraint(x, pltpu.HBM)


def in_vmem(x):
    return pltpu.with_memory_space_constraint(x, pltpu.VMEM)


def run(copies):
    for c in copies:
        c.start()
    for c in copies:
        c.wait()


def piece_copies(c_ref, o_ref, sems, i, parts=2):
    rows = o_ref.shape[0]
    step = rows // parts
    return [
        pltpu.make_async_copy(
            c_ref.at[pl.ds(i * rows + p * step, step)],
            o_ref.at[pl.ds(p * step, step)],
            sems.at[p],
        )
        for p in range(parts)
    ]


def load_pieces(chol, first, count, piece, after):
    def body(c_ref, _, *refs):
        run([c for j in range(count) for c in piece_copies(c_ref, refs[j], refs[count].at[j], first + j)])

    return call(
        body,
        [piece] * count,
        in_hbm(chol),
        after,
        flops=count * 2 * 10**9,
        ins=[HBM, HBM],
        scratch=[pltpu.SemaphoreType.DMA((count, 2))],
    )


def transposed(piece, *after):
    rows, cols = piece.shape
    tile = min(512, rows, cols)

    def body(c, *refs):
        o = refs[-1]

        @pl.loop(0, rows // tile)
        def _(r):
            at = pl.ds(pl.multiple_of(r * tile, tile), tile)
            for j in range(cols // tile):
                o[j * tile : (j + 1) * tile, at] = c[at, j * tile : (j + 1) * tile].T

    return call(
        body, pltpu.VMEM((cols, rows), bf16), piece, *after, mib=2, ins=[VMEM] + [HBM] * len(after)
    )


def ids():
    blk, grp = lax.axis_index("blk"), lax.axis_index("grp")
    return blk, grp // 2, grp % 2


def role(p, core):
    return jnp.where(core == 0, p, (p >> 1) | ((p & 1) << 1))


def fast(green, chol, aux):
    wb, depth = green.shape
    width = chol.shape[1]
    wg = aux.shape[0]
    half = width // 2
    n_chunks = depth // width
    n_pieces, rows = 2 * n_chunks, width // 2
    piece = pltpu.VMEM((rows, width), bf16)
    tile = min(256, half)

    near = cross(green, 0)

    def begin(c_ref, aux_ref, g_ref, c0_ref, c1_ref, kept_ref, sent_ref, own_ref, sems):
        _, _, core = ids()
        at = [pl.ds(pl.multiple_of(c * half, half), half) for c in (core, 1 - core)]
        run(
            [
                pltpu.make_async_copy(aux_ref.at[:, at[0]], kept_ref, sems.at[2, 0]),
                pltpu.make_async_copy(aux_ref.at[:, at[1]], sent_ref, sems.at[2, 1]),
                pltpu.make_async_copy(g_ref, own_ref, sems.at[3, 0]),
            ]
            + piece_copies(c_ref, c0_ref, sems.at[0], 0)
            + piece_copies(c_ref, c1_ref, sems.at[1], 1)
        )

    c0, c1, aux_kept, aux_sent, own = call(
        begin,
        (
            piece,
            piece,
            struct((wg, half), bf16),
            struct((wg, half), bf16),
            pltpu.VMEM((wb, depth), bf16),
        ),
        in_hbm(chol), in_hbm(aux), in_hbm(green),
        flops=4 * 10**9,
        ins=[HBM] * 3,
        scratch=[pltpu.SemaphoreType.DMA((4, 2))],
    )
    side, far = cross(own, 1), cross(near, 1)
    pieces = [c0, c1, *load_pieces(chol, 2, n_pieces - 4, piece, aux_kept)]
    aux_got = swap(aux_sent, "grp", 1)

    def bias_half(all_ref, c_refs, offset, start=0):
        for n in range(0, half, tile):
            total = None
            for k, c in enumerate(c_refs, start):
                term = jnp.dot(
                    all_ref[:, k * rows : (k + 1) * rows],
                    c[:, pl.ds(pl.multiple_of(offset + n, tile), tile)],
                    preferred_element_type=f32,
                )
                total = term if total is None else total + term
            yield slice(n, n + tile), total

    early = n_chunks
    here = n_pieces - 2

    def first(*refs):
        parts, c_refs, c_ref = refs[:4], refs[4 : 4 + here], refs[4 + here]
        all_ref, sent_ref, part_ref, *last_refs, sems, total_ref = refs[5 + here :]
        copies = [
            c for j, r in enumerate(last_refs) for c in piece_copies(c_ref, r, sems.at[j], here + j)
        ]
        for c in copies:
            c.start()
        blk, _, core = ids()

        @pl.when(core < 2)
        def _():
            for p in range(4):
                at = pl.ds(p * PAD, wb)
                all_ref[at, :] = parts[p][...]
                all_ref[pl.ds(p * PAD + wb, PAD - wb), :] = jnp.zeros((PAD - wb, depth), bf16)
            for at, total in bias_half(all_ref, c_refs[:early], core * half):
                part_ref[:, at] = total
            for at, total in bias_half(all_ref, c_refs, (1 - core) * half):
                total_ref[:, at] = total

        for c in copies[:2]:
            c.wait()
        for at, total in bias_half(all_ref, last_refs[:1], (1 - core) * half, here):
            total_ref[:, at] += total
        for c in copies[2:]:
            c.wait()
        for at, total in bias_half(all_ref, last_refs[1:], (1 - core) * half, here + 1):
            total += total_ref[:, at]
            for p in range(4):
                sent_ref[blk ^ role(p, core), :, at] = total[p * PAD : p * PAD + wb].astype(bf16)

    flops1 = 2 * 128 * depth * half
    g_all, sent, part, *last = call(
        first,
        (
            struct((4 * PAD, depth), bf16),
            struct((4, wb, half), bf16),
            struct((4 * PAD, half), f32),
            piece,
            piece,
        ),
        own, near, side, far, *pieces, in_hbm(chol),
        flops=flops1,
        ins=[VMEM] * (4 + here) + [HBM],
        scratch=[pltpu.SemaphoreType.DMA((2, 2)), pltpu.VMEM((4 * PAD, half), f32)],
    )
    pieces += last
    other = swap(sent, "grp", 1)

    def second(all_ref, part_ref, *refs):
        c_refs, out_ref = refs[:-1], refs[-1]
        blk, _, core = ids()
        for at, total in bias_half(all_ref, c_refs, core * half, early):
            total += part_ref[:, at]
            for p in range(4):
                out_ref[blk ^ role(p, core), :, at] = total[p * PAD : p * PAD + wb]

    mine = call(second, struct((4, wb, half), f32), g_all, part, *pieces[early:], flops=flops1)

    def combine(mine_ref, other_ref, keep_ref, *sent_refs):
        _, z, _ = ids()
        keep_ref[...] = mine_ref[z] + other_ref[z].astype(f32)
        for t, s in zip((2, 3, 1), sent_refs):
            s[...] = (mine_ref[z ^ t] + other_ref[z ^ t].astype(f32)).astype(bf16)

    keep, *sums = call(
        combine, (struct((wb, half), f32),) + (struct((wb, half), bf16),) * 3, mine, other
    )
    sums = [swap(s, "grp", 2 * t) for t, s in zip((2, 3, 1), sums)]
    turned = []
    for k in range(3):
        turned.append(
            transposed(pieces[k], turned[-1] if turned else keep, *pieces[k + 1 :])
        )

    def shift(keep_ref, r1, r2, r3, aux_ref, got_ref, _, bias_ref, give_ref, out_ref):
        _, _, core = ids()
        bias = keep_ref[...]
        for r in (r1, r2, r3):
            bias = bias + r[...].astype(f32)
        bias_ref[...] = bias
        give_ref[...] = jnp.where(core == 0, bias[wg:], bias[:wg])
        own = aux_ref[...].astype(f32)
        got = got_ref[...].astype(f32)
        top = jnp.where(core == 0, own, got)
        low = jnp.where(core == 0, got, own)
        out_ref[...] = (jnp.concatenate([top, low], 0) + tau_root * bias).astype(bf16)

    bias, give, shifted = call(
        shift,
        (struct((wb, half), f32), struct((wg, half), f32), struct((wb, half), bf16)),
        keep, *sums, aux_kept, aux_got, turned[-1],
        ins=[VMEM] * 6 + [HBM],
    )
    for k in range(3, 5):
        turned.append(transposed(pieces[k], shifted if k == 3 else turned[-1], *pieces[k + 1 :]))
    blocks = [shifted] + [swap(shifted, "grp", 2 * t) for t in (1, 2, 3)]
    bias_got = swap(give, "grp", 1)

    def arrange(*refs):
        ins, out_ref = refs[:4], refs[5]
        blk, z, _ = ids()
        for t in range(4):
            out_ref[z ^ t ^ blk, :wb] = ins[t][...]
            out_ref[t, wb:] = jnp.zeros((PAD - wb, half), bf16)

    s_mine = call(arrange, struct((4, PAD, half), bf16), *blocks, turned[-1], ins=[VMEM] * 4 + [HBM])
    s_other = swap(s_mine, "grp", 1)

    n_first = n_pieces // 2
    groups = [range(n_first), range(n_first, n_pieces - 2), range(n_pieces - 2, n_pieces)]

    def placed(all_ref, ref, start):
        _, _, core = ids()
        for p in range(4):
            all_ref[p * PAD : (p + 1) * PAD, pl.ds(start, half)] = ref[role(p, core)]

    def tiles(c_refs):
        return [
            (c, n, slice(j * rows + n, j * rows + n + tile))
            for j, c in enumerate(c_refs)
            for n in range(0, rows, tile)
        ]

    def stored(total, at, s_ref, pass_ref, own_ref):
        block = [total[p * PAD : p * PAD + wb] for p in range(4)]
        own_ref[:, at] = block[0]
        pass_ref[:, at] = block[1]
        s_ref[0, :, at] = block[3].astype(bf16)
        s_ref[1, :, at] = block[2].astype(bf16)

    def field_mine(mine_ref, *refs):
        c_refs, (part_ref, all_ref) = refs[:-2], refs[-2:]
        _, _, core = ids()
        placed(all_ref, mine_ref, 0)
        k = pl.ds(pl.multiple_of(core * half, half), half)
        for c, n, at in tiles(c_refs):
            part_ref[:, at] = jnp.dot(all_ref[...], c[k, n : n + tile], preferred_element_type=f32)

    def field_other(other_ref, part_ref, *refs):
        c_refs, (*outs, all_ref) = refs[:-4], refs[-4:]
        _, _, core = ids()
        placed(all_ref, other_ref, 0)
        k = pl.ds(pl.multiple_of((1 - core) * half, half), half)
        for c, n, at in tiles(c_refs):
            total = jnp.dot(all_ref[...], c[k, n : n + tile], preferred_element_type=f32)
            stored(part_ref[:, at] + total, at, *outs)

    def field(group, mine_ref, other_ref, *refs):
        c_refs, (*outs, all_ref) = refs[: len(group)], refs[-4:]
        _, _, core = ids()
        placed(all_ref, mine_ref, pl.multiple_of(core * half, half))
        placed(all_ref, other_ref, pl.multiple_of((1 - core) * half, half))
        for c, n, at in tiles(c_refs):
            if group.start + at.start // rows < len(turned):
                total = jnp.dot(all_ref[...], c[:, n : n + tile], preferred_element_type=f32)
            else:
                total = lax.dot_general(
                    c[n : n + tile, :], all_ref[...], (((1,), (1,)), ((), ())), preferred_element_type=f32
                ).T
            stored(total, at, *outs)

    def outs(group):
        n = len(group) * rows
        return struct((2, wb, n), bf16), struct((wb, n), f32), struct((wb, n), f32)

    some = [pltpu.VMEM((4 * PAD, half), bf16)]
    whole = [pltpu.VMEM((4 * PAD, width), bf16)]
    part = call(
        field_mine,
        struct((4 * PAD, n_first * rows), f32),
        s_mine, *turned[:n_first],
        scratch=some,
    )

    def later(group, after):
        n = len(group)
        return call(
            functools.partial(field, group),
            outs(group),
            s_mine, s_other, *(turned + pieces[len(turned) :])[group.start : group.stop], after,
            flops=4 * 128 * width * width,
            ins=[VMEM] * (2 + n) + [HBM],
            scratch=whole,
        )

    middle = later(groups[1], s_mine)
    last = later(groups[2], middle[2])
    opening = call(
        field_other,
        outs(groups[0]),
        s_other, part, *turned[:n_first],
        flops=4 * 128 * width * width,
        scratch=some,
    )
    stage = []
    for sent, passed, mine in (last, middle, opening):
        stage.append((cross(sent, 1), passed, mine))

    def forward(*refs):
        out_ref, new_ref = refs[-2:]
        start = 0
        for j in range(len(refs) // 3):
            got_ref, pass_ref, own_ref = refs[3 * j : 3 * j + 3]
            at = pl.ds(start, own_ref.shape[1])
            start += own_ref.shape[1]
            out_ref[:, at] = (pass_ref[...] + got_ref[0].astype(f32)).astype(bf16)
            new_ref[:, at] = own_ref[...] + got_ref[1].astype(f32)

    done = []
    for part in (stage[1:][::-1], stage[:1]):
        n = sum(s[2].shape[1] for s in part)
        sent, mine = call(
            forward, (struct((wb, n), bf16), struct((wb, n), f32)), *[r for s in part for r in s]
        )
        done += [mine, cross(sent, 0)]

    def written(start, mine_ref, got_ref, *refs):
        out_ref, whole_ref, sem = refs[-3:]
        n = mine_ref.shape[1]
        whole_ref[...] = (mine_ref[...] + got_ref[...].astype(f32)).astype(bf16)
        run([pltpu.make_async_copy(whole_ref, out_ref.at[:, pl.ds(start, n)], sem)])

    def write(start, mine, got, *old):
        return pl.pallas_call(
            functools.partial(written, start),
            out_shape=struct((wb, depth), bf16),
            in_specs=[VMEM] * 2 + [HBM] * len(old),
            out_specs=HBM,
            scratch_shapes=[pltpu.VMEM(mine.shape, bf16), pltpu.SemaphoreType.DMA],
            input_output_aliases={2: 0} if old else {},
            compiler_params=pltpu.CompilerParams(vmem_limit_bytes=3 << 20),
        )(mine, got, *old)

    result = write(0, *done[:2])
    result = write(done[0].shape[1], *done[2:], result)

    def own_bias(bias_ref, got_ref, out_ref):
        _, _, core = ids()
        b = bias_ref[...]
        out_ref[:, pl.ds(pl.multiple_of(core * half, half), half)] = jnp.where(
            core == 0, b[:wg], b[wg:]
        )
        out_ref[:, pl.ds(pl.multiple_of((1 - core) * half, half), half)] = got_ref[...]

    bias_own = call(own_bias, struct((wg, width), f32), bias, bias_got)
    return bias_own, result


def solution(mesh):
    blk, grp = mesh.shape["blk"], mesh.shape["grp"]

    def local(green, chol, aux):
        plane = blk == 4 and grp == 8
        fits = chol.shape[0] % (2 * chol.shape[1]) == 0 and green.shape[0] == 2 * aux.shape[0]
        return (fast if plane and fits and green.shape[0] <= PAD else general)(green, chol, aux)

    placed = (P("blk", "grp"), P("grp", "blk"), P("grp", "blk"))
    return jax.shard_map(
        local,
        mesh=mesh,
        in_specs=placed,
        out_specs=(P("grp", "blk"), P("blk", "grp")),
        check_vma=False,
    )
```
